256 devices in a mesh: sect: 4 (over x), node: 64 (over z, y, core).
Axes of the slice: x: 4, y: 4, z: 8, core: 2. Of those that a mesh axis runs over, the one named last changes fastest.
Arguments:
- grid_feat: bfloat16 [65536, 512], P(('sect', 'node')), may hold values from -6 to 6
- edge_len: float32 [65536, 2], P(('sect', 'node')), may hold values from 0.2 to 1.5
- g2m_owner: int32 [65536, 2], P(('sect', 'node')), may hold values from 0 to 63, all different within a row; in each aligned block of 256 rows (0 to 255, 256 to 511, ...) at most 16 rows name the same one
- g2m_dst: int32 [65536, 2], P(('sect', 'node')), may hold values from 0 to 511
- enc_weight: bfloat16 [512, 512], replicated, may hold values from -0.25 to 0.25
- enc_vec: float32 [512], replicated, may hold values from -5 to 5
- mesh_init: bfloat16 [64, 512, 512], P('node', 'sect'), may hold values from -1.11 to 1.11
- mesh_weight: bfloat16 [512, 512], replicated, may hold values from -0.015625 to 0.015625
- halo_send: int32 [4, 64, 4, 64, 2], P('sect', 'node'), may hold values from 0 to 127
- mesh_src: int32 [64, 512, 8], P('node', 'sect'), may hold values from 0 to 639
- proc_weight: bfloat16 [2, 4, 512, 512], replicated, may hold values from -0.25 to 0.25
- cot: bfloat16 [64, 512, 512], P('node', 'sect'), may hold values from -16 to 16
Outputs:
- mesh_out: bfloat16 [64, 512, 512], P('node', 'sect')
- grid_grad: bfloat16 [65536, 512], P(('sect', 'node'))
The draws below stay inside these ranges and needn't reach their ends.
Inputs may be any that keep to these rules, and one draw needn't show every extreme that they name: `g2m_owner`: within the 256 grid nodes of one device (aligned blocks), at most 16 edges name one mesh block, and some block is named by exactly 16 edges in some or all devices; the 2 edges of one grid node name different blocks. `mesh_src`: entries below 128 name own rows of the table, the others received rows.
All inputs are finite; a program needn't handle non-finite values.
Results may differ from the reference program's by a relative error of at most 0.009.
Values may be sent and summed in bfloat16 or wider, within the bound.
A program may use at most 64 MiB of HBM per device.

```python
import math
import jax
import jax.numpy as jnp
import numpy as np
from jax import lax

D = 512
G_DEV = 256
Q_DEV = 128
KG = 2
KM = 8
HCAP = 2
LAYERS = 2
OWNERS = 64
SECTIONS = 4
M_DEV = 512
MESH = 32768
GRID = 65536
CAP = 16
TABLE = 640
N_SECT = 4
N_NODE = 64


def draw_mesh_init(key, part):
    key = jax.random.fold_in(key, 11)
    key_rows, key_vals = jax.random.split(key)
    row_scale = jnp.exp(jax.random.uniform(key_rows, (OWNERS, M_DEV, 1), jnp.float32, -3.0, -1.0))
    values = jnp.clip(jax.random.normal(key_vals, (OWNERS, M_DEV, D), jnp.float32), -3.0, 3.0)
    return (row_scale * values).astype(jnp.bfloat16)


def place_ends(entries, own_key, least, high):
    longest = entries.shape.index(max(entries.shape))
    spots = []
    for shift in (0, 1):
        where = [jax.random.randint(jax.random.fold_in(own_key, axis), (), 0, length) for axis, length in enumerate(entries.shape)]
        where[longest] = (where[longest] + shift) % entries.shape[longest]
        spots.append(tuple(where))
    return entries.at[spots[0]].set(least).at[spots[1]].set(high)


def level_of(own_key, shape, pieces, low, largest):
    level = 1.0
    for axis_at, blocks in pieces:
        steps = jax.random.uniform(jax.random.fold_in(jax.random.fold_in(own_key, 6), axis_at), (blocks,), jnp.float32, low / len(pieces), largest / len(pieces))
        level = level * jnp.repeat(jnp.exp(steps), shape[axis_at] // blocks).reshape((-1,) + (1,) * (len(shape) - 1 - axis_at))
    return level


def deal_out(rng, own, number, rows, count, top, most, skew):
    sequence = jax.random.permutation(rng, count)
    heavy_load, usual = shares(count, rows * top, most, skew, True), shares(count, rows * top, most, skew, False)
    places = jnp.arange(count)

    def named(sizes, turn):
        used = int((sizes > 0).sum())
        fixed = max(1, used // 4)
        passed = fixed + (places - fixed + turn * (used - fixed)) % max(1, count - fixed)
        return jnp.zeros((count,), jnp.int32).at[sequence[jnp.where(places < fixed, places, passed)]].set(jnp.asarray(sizes, jnp.int32))

    sizes = jnp.where(number % 4 == 0, named(heavy_load, number // 4), named(usual, number - number // 4 - 1))
    mixed = jax.random.permutation(jax.random.fold_in(own, 3), count)
    source_of, sink = mixed[0:count // 2 * 2:2], mixed[1:count // 2 * 2:2]
    margin = jnp.minimum(sizes[source_of] - 1, most - sizes[sink]) // 2
    margin = jnp.where((source_of == sequence[0]) | (sink == sequence[0]) | (sizes[sink] == 0), 0, jnp.maximum(margin, 0))
    passed = jax.random.randint(jax.random.fold_in(own, 4), (count // 2,), 0, 1 << 20) % (margin + 1)
    sizes = sizes.at[source_of].add(-passed).at[sink].add(passed)
    members = jnp.searchsorted(jnp.cumsum(sizes), jnp.arange(rows * top), side="right").astype(jnp.int32)
    listing = members.reshape(top, rows).T
    listing = listing[jax.random.permutation(jax.random.fold_in(own, 1), rows)]
    turn = jax.random.randint(jax.random.fold_in(own, 2), (rows, 1), 0, top)
    return jnp.take_along_axis(listing, (jnp.arange(top)[None, :] + turn) % top, axis=1)


def shares(amount, total, bound, skew, full):
    weights = [(1 << 20) // math.isqrt(standing ** skew) + 1 for standing in range(1, amount + 1)]
    largest = bound if full else min(bound, max(-(-total // amount), total * weights[0] // sum(weights)))
    least = 1 if total - largest >= amount - 1 else 0
    holding, rest = [largest] + [least] * (amount - 1), total - largest - least * (amount - 1)
    while rest > 0:
        free = [i for i in range(1, amount) if holding[i] < largest] or [i for i in range(1, amount) if holding[i] < bound]
        whole, left = sum([weights[i] for i in free]), rest
        for i in free:
            more = min(bound - holding[i], max(1, left * weights[i] // whole), rest)
            holding[i] = holding[i] + more
            rest = rest - more
    return np.array(holding)


def normal_values(own_key, dims, width, most, shards=(), kind=jnp.bfloat16):
    entries = jax.random.normal(own_key, dims, jnp.float32) * width
    if len(shards) > 0:
        entries = level_of(own_key, dims, shards, -0.22, 0.18) * entries
    return jnp.clip(entries, min=-most, max=most).astype(kind)


def setup_inputs(seed: int = 0) -> dict:
    splits = jax.random.split(jax.random.key(seed), 13)
    grid_feat = normal_values(splits[0], (GRID, D), 1.0, 6.0, ((0, 256),))
    edge_len = jnp.clip(0.2 + 1.3 * jax.random.uniform(splits[1], (GRID, KG), jnp.float32) ** level_of(splits[1], (GRID, KG), ((0, 256),), -0.2, 0.2), 0.2, 1.5)
    g2m_owner_keys = jax.random.split(jax.random.fold_in(splits[2], 1), GRID // G_DEV)
    g2m_owner_turns = jax.random.permutation(jax.random.fold_in(splits[2], 3), GRID // G_DEV)
    g2m_owner = jax.vmap(lambda own, number: deal_out(jax.random.fold_in(splits[2], 2), own, number, G_DEV, OWNERS, KG, CAP, 1))(g2m_owner_keys, g2m_owner_turns).reshape((GRID, KG))
    g2m_dst = place_ends(jax.random.randint(splits[3], (GRID, KG), 0, M_DEV), jax.random.fold_in(splits[3], 1), 0, M_DEV - 1).astype(jnp.int32)
    enc_weight = normal_values(splits[4], (D, D), D ** -0.5, 0.25)
    enc_vec = normal_values(splits[5], (D,), 1.0, 5.0, (), jnp.float32)
    mesh_init = draw_mesh_init(jax.random.fold_in(splits[12], 71), 0)
    mesh_weight = normal_values(splits[7], (D, D), (256 * D) ** -0.5, 0.015625)
    halo_send = place_ends(jax.random.randint(splits[8], (SECTIONS, OWNERS, SECTIONS, OWNERS, HCAP), 0, Q_DEV), jax.random.fold_in(splits[8], 1), 0, Q_DEV - 1).astype(jnp.int32)
    mesh_src = place_ends(jax.random.randint(splits[9], (OWNERS, M_DEV, KM), 0, TABLE), jax.random.fold_in(splits[9], 1), 0, TABLE - 1).astype(jnp.int32)
    proc_weight = normal_values(splits[10], (LAYERS, 4, D, D), D ** -0.5, 0.25)
    cot = normal_values(splits[11], (OWNERS, M_DEV, D), 4.0, 16.0, ((0, 64), (1, 4)))
    return dict(grid_feat=grid_feat, edge_len=edge_len, g2m_owner=g2m_owner, g2m_dst=g2m_dst, enc_weight=enc_weight, enc_vec=enc_vec, mesh_init=mesh_init, mesh_weight=mesh_weight, halo_send=halo_send, mesh_src=mesh_src, proc_weight=proc_weight, cot=cot)


HIGH = lax.Precision.HIGHEST

def to_low(value):
    rounded = lax.optimization_barrier(value.astype(jnp.bfloat16)).astype(jnp.float32)
    return value + lax.stop_gradient(rounded - value)

def matmul(left, right):
    return jnp.matmul(left, right, precision=HIGH)

def layer_norm(value):
    mean = lax.optimization_barrier(jnp.mean(value, axis=-1, keepdims=True))
    centred = value - mean
    var = lax.optimization_barrier(jnp.mean(centred * centred, axis=-1, keepdims=True))
    return centred * lax.rsqrt(var + 1e-05)

def pick_rows(rows, picks):
    return rows[picks]

def sect_layer(state, incoming, sources, weights):
    table = jnp.concatenate([state, incoming], axis=1)
    from_src = matmul(table, weights[0])
    to_dst = matmul(state, weights[1])
    joined = jax.vmap(pick_rows)(from_src, sources) + to_dst[:, :, None, :]
    agg = to_low(lax.optimization_barrier(jnp.sum(jax.nn.silu(joined), axis=2)))
    mixed = matmul(state, weights[2]) + matmul(agg, weights[3])
    return to_low(state + jax.nn.silu(layer_norm(mixed)))

def forward(grid, edge_len, g2m_owner, g2m_dst, enc_weight, enc_vec, mesh_init, mesh_weight, halo_send, mesh_src, proc_weight):
    pre = matmul(grid, enc_weight)
    message = to_low(jax.nn.silu(pre[:, None, :] + edge_len[:, :, None] * enc_vec))
    target = (g2m_owner * M_DEV + g2m_dst).reshape(-1).astype(jnp.int32)
    agg = jax.ops.segment_sum(message.reshape(-1, D), target, num_segments=MESH)
    mesh_pre = matmul(to_low(agg), mesh_weight)
    state = to_low(mesh_init.reshape(MESH, D) + jax.nn.silu(mesh_pre))
    state = state.reshape(N_NODE, N_SECT, Q_DEV, D).transpose(1, 0, 2, 3)
    sources = mesh_src.reshape(N_NODE, N_SECT, Q_DEV, KM).transpose(1, 0, 2, 3)
    picks = halo_send.reshape(N_SECT, N_NODE, N_SECT * N_NODE * HCAP)
    for layer in range(LAYERS):
        weights = proc_weight[layer]
        outgoing = jax.vmap(jax.vmap(pick_rows))(state, picks)
        outgoing = outgoing.reshape(N_SECT, N_NODE, N_SECT, N_NODE, HCAP, D)
        incoming = outgoing.transpose(2, 3, 0, 1, 4, 5).reshape(N_SECT, N_NODE, N_SECT * N_NODE * HCAP, D)

        def one_sect(item):
            return sect_layer(item[0], item[1], item[2], weights)
        state = lax.map(one_sect, (state, incoming, sources))
    return state.transpose(1, 0, 2, 3).reshape(N_NODE, M_DEV, D)

def reference(grid_feat, edge_len, g2m_owner, g2m_dst, enc_weight, enc_vec, mesh_init, mesh_weight, halo_send, mesh_src, proc_weight, cot):

    def run(grid):
        return forward(grid, edge_len.astype(jnp.float32), g2m_owner, g2m_dst, enc_weight.astype(jnp.float32), enc_vec.astype(jnp.float32), mesh_init.astype(jnp.float32), mesh_weight.astype(jnp.float32), halo_send, mesh_src, proc_weight.astype(jnp.float32))
    mesh_out, pull = jax.vjp(run, grid_feat.astype(jnp.float32))
    grid_grad = pull(cot.astype(jnp.float32))[0]
    return (mesh_out.astype(jnp.bfloat16), grid_grad.astype(jnp.bfloat16))
```

```python
import functools

import jax
import jax.numpy as jnp
from jax import lax
from jax.experimental import pallas as pl
from jax.experimental.pallas import tpu as pltpu
from jax.sharding import PartitionSpec as P

MESH = pl.DeviceIdType.MESH
F32 = jnp.float32
BF16 = jnp.bfloat16
NN = ((1,), (0,))
NT = ((1,), (1,))
TN = ((0,), (0,))
LANES = 128
CHUNKS = 2


def dot(left, right, dims=NN):
    return lax.dot_general(left, right, (dims, ((), ())), preferred_element_type=F32)


def iota(shape, dim):
    return lax.broadcasted_iota(jnp.int32, shape, dim)


def slope_of(value, sig):
    return sig * (1.0 + value * (1.0 - sig))


def fused(
    sects,
    nodes,
    feat,
    length,
    owner,
    dest,
    enc_w,
    vec,
    init,
    mesh_w,
    sends,
    sources,
    proc_w,
    cot,
    mesh_out,
    grid_grad,
    dst_out,
    dst_in,
    msg_out,
    msg_in,
    part_out,
    part_in,
    halo_out,
    halo_in,
    back_out,
    back_in,
    gath_out,
    gath_in,
    slot_out,
    slot_in,
    pick,
    scat,
    edge_pick,
    act_slope,
    joined,
    far_part,
    far_grad,
    piece,
    last_part,
    send_sem,
    recv_sem,
):
    sect = lax.axis_index("sect")
    node = lax.axis_index("node")
    world = sects * nodes
    zero = lax.div(sect, sects)
    line = sect * nodes + node
    grid_rows, fanout = length.shape
    block, degree = sources.shape
    width = feat.shape[1]
    whole = block * sects
    cap = msg_out.shape[2]
    slots = nodes * cap
    chunks = msg_out.shape[0]
    part = width // chunks
    layers = proc_w.shape[0]
    fan = halo_out.shape[2]
    halo = world * fan

    barrier = pltpu.get_barrier_semaphore()

    def greet_node(step, carry):
        peer = lax.rem(node + step, nodes)
        pl.semaphore_signal(barrier, inc=1, device_id=(sect, peer), device_id_type=MESH)
        return carry

    def greet_sect(step, carry):
        peer = lax.rem(sect + step, sects)
        pl.semaphore_signal(barrier, inc=1, device_id=(peer, node), device_id_type=MESH)
        return carry

    lax.fori_loop(1, nodes, greet_node, 0)
    lax.fori_loop(1, sects, greet_sect, 0)

    def push(src, dst, at, device):
        pltpu.make_async_remote_copy(
            src_ref=src,
            dst_ref=dst,
            send_sem=send_sem.at[at],
            recv_sem=recv_sem.at[at],
            device_id=device,
            device_id_type=MESH,
        ).start()

    def over_nodes(src, dst, at):
        def step(off, carry):
            peer = lax.rem(node + off, nodes)
            push(src.at[peer], dst.at[node], at, (sect, peer))
            return carry

        lax.fori_loop(1, nodes, step, 0, unroll=9)

    def over_all(src, dst, at):
        def step(off, carry):
            peer = lax.rem(line + off, world)
            push(
                src.at[peer],
                dst.at[line],
                at,
                (lax.div(peer, nodes), lax.rem(peer, nodes)),
            )
            return carry

        lax.fori_loop(1, world, step, 0, unroll=15)

    def landed(ref, count, sem):
        some = ref.at[pl.ds(0, count)]
        pltpu.make_async_copy(some, some, sem).wait()

    at_dst = 0
    at_msg = 1
    at_part = at_msg + chunks
    at_halo = at_part + chunks
    at_back = at_halo + layers
    at_gath = at_back + layers
    at_slot = at_gath + chunks

    upper = (iota((grid_rows, grid_rows), 0) < iota((grid_rows, grid_rows), 1)).astype(BF16)
    used = jnp.zeros((nodes, 1), F32)
    table = jnp.zeros((nodes, LANES), F32)
    for k in range(fanout):
        own_row = owner[k : k + 1, :]
        dst_row = dest[k : k + 1, :]
        hot = (iota((nodes, grid_rows), 0) == own_row).astype(F32)
        before = dot(hot.astype(BF16), upper) + used
        rank = jnp.sum(hot * before, axis=0, keepdims=True).astype(jnp.int32)
        used = used + jnp.sum(hot, axis=1, keepdims=True)
        place = own_row * cap + rank
        pick[:, k * grid_rows : (k + 1) * grid_rows] = (
            iota((slots, grid_rows), 0) == place
        ).astype(BF16)
        level = (iota((LANES, grid_rows), 0) == rank).astype(BF16)
        high = (hot * (dst_row >> 4).astype(F32)).astype(BF16)
        low = (hot * ((dst_row & 15) + 1).astype(F32)).astype(BF16)
        table = table + 16.0 * dot(high, level, NT) + dot(low, level, NT)
    dst_out[...] = table.reshape(nodes, 1, LANES)

    pre = dot(feat[...], enc_w[...])
    acts = [pre + length[:, k : k + 1] * vec[...] for k in range(fanout)]
    sigs = [jax.nn.sigmoid(act) for act in acts]
    message = jnp.concatenate(
        [(act * sig).astype(BF16) for act, sig in zip(acts, sigs)], axis=0
    )

    pl.semaphore_wait(barrier, nodes + sects - 2)
    over_nodes(dst_out, dst_in, at_dst)
    dst_in[node] = dst_out[node]
    for c in range(chunks):
        cols = slice(c * part, (c + 1) * part)
        msg_out[c] = dot(pick[...], message[:, cols]).astype(BF16).reshape(nodes, cap, part)
        over_nodes(msg_out.at[c], msg_in.at[c], at_msg + c)
        msg_in[c, node] = msg_out[c, node]

    for k in range(fanout):
        act_slope[k] = slope_of(acts[k], sigs[k])

    for k in range(degree):
        edge_pick[k * block : (k + 1) * block, :] = (
            iota((block, block + halo), 1) == sources[:, k : k + 1]
        ).astype(BF16)
    halo_pick = (iota((block, halo), 0) == sends[...]).astype(BF16)

    landed(dst_in, nodes - 1, recv_sem.at[at_dst])
    got = dst_in[...].reshape(nodes, LANES)
    got_high = jnp.floor(got * (1.0 / 16.0))
    got_low = got - 16.0 * got_high
    spread = (lax.rem(iota((LANES, slots), 1), cap) == iota((LANES, slots), 0)).astype(BF16)
    mine = (lax.div(iota((nodes, slots), 1), cap) == iota((nodes, slots), 0)).astype(F32)
    wide = 16.0 * dot(got_high.astype(BF16), spread) + dot(got_low.astype(BF16), spread)
    got_row = jnp.sum(wide * mine, axis=0, keepdims=True).astype(jnp.int32) - 1
    scat[...] = (iota((whole, slots), 0) == got_row).astype(BF16)

    mesh_pre = jnp.zeros((block, width), F32)
    own_part = []
    for c in range(chunks):
        landed(msg_in.at[c], nodes - 1, recv_sem.at[at_msg + c])
        agg = dot(scat[...], msg_in[c].reshape(slots, part))
        part_out[c] = agg.astype(BF16).reshape(sects, block, part)
        for off in range(1, sects):
            peer = lax.rem(sect + off, sects)
            push(part_out.at[c, peer], part_in.at[c, sect], at_part + c, (peer, node))
        part_in[c, sect] = part_out[c, sect]
    for c in range(chunks):
        landed(part_in.at[c], sects - 1, recv_sem.at[at_part + c])
        total = jnp.sum(part_in[c].astype(F32), axis=0)
        last_part[c, :block, :] = dot(total.astype(BF16), mesh_w[c * part : (c + 1) * part, :])
    for c in range(chunks):
        mesh_pre = mesh_pre + last_part[zero + c, :block, :]
    mesh_sig = jax.nn.sigmoid(mesh_pre)
    state = (init[...].astype(F32) + mesh_pre * mesh_sig).astype(BF16)

    saved = []
    for layer in range(layers):
        out = dot(halo_pick, state, TN).astype(BF16)
        halo_out[layer] = out.reshape(world, fan, width)
        over_all(halo_out.at[layer], halo_in.at[layer], at_halo + layer)
        halo_in[layer, line] = halo_out[layer, line]
        near = dot(edge_pick[:, :block], state).astype(BF16)
        piece[2] = dot(state, proc_w[layer, 1])
        joined[layer] = dot(near, proc_w[layer, 0])
        piece[1] = dot(state, proc_w[layer, 2])
        if layer > 0:
            prev = joined[layer - 1]
            joined[layer - 1] = slope_of(prev, jax.nn.sigmoid(prev))
        landed(halo_in.at[layer], world - 1, recv_sem.at[at_halo + layer])
        far = dot(edge_pick[:, block:], halo_in[layer].reshape(halo, width)).astype(BF16)
        far_part[...] = dot(far, proc_w[layer, 0])
        agg = jnp.zeros((block, width), F32)
        to_dst = piece[zero + 2]
        for k in range(degree):
            rows = slice(k * block, (k + 1) * block)
            full = joined[zero + layer, rows, :] + far_part[rows, :] + to_dst
            joined[layer, rows, :] = full
            agg = agg + full * jax.nn.sigmoid(full)
        agg = agg.astype(BF16)
        piece[0] = dot(agg, proc_w[layer, 3])
        mixed = piece[zero + 1] + piece[zero]
        centred = mixed - jnp.mean(mixed, axis=1, keepdims=True)
        scale = lax.rsqrt(jnp.mean(centred * centred, axis=1, keepdims=True) + 1e-05)
        normed = centred * scale
        sig = jax.nn.sigmoid(normed)
        saved.append((normed, scale, slope_of(normed, sig)))
        state = (state.astype(F32) + normed * sig).astype(BF16)
    mesh_out[...] = state
    last = joined[layers - 1]
    joined[layers - 1] = slope_of(last, jax.nn.sigmoid(last))

    grad = cot[...].astype(F32)
    for layer in reversed(range(layers)):
        normed, scale, slope = saved[layer]
        grad_normed = grad * slope
        grad_mixed = scale * (
            grad_normed
            - jnp.mean(grad_normed, axis=1, keepdims=True)
            - normed * jnp.mean(grad_normed * normed, axis=1, keepdims=True)
        )
        grad_mixed = grad_mixed.astype(BF16)
        grad_agg = dot(grad_mixed, proc_w[layer, 3], NT)
        grad_dst = jnp.zeros((block, width), F32)
        for k in range(degree):
            rows = slice(k * block, (k + 1) * block)
            grad_joined = joined[layer, rows, :] * grad_agg
            grad_dst = grad_dst + grad_joined
            far_grad[rows, :] = grad_joined.astype(BF16)
        grad_dst = grad_dst.astype(BF16)
        out = dot(edge_pick[:, block:], far_grad[...], TN).astype(BF16)
        back_out[layer] = out.reshape(world, fan, width)
        over_all(back_out.at[layer], back_in.at[layer], at_back + layer)
        back_in[layer, line] = back_out[layer, line]
        piece[0] = dot(grad_mixed, proc_w[layer, 2], NT)
        piece[1] = dot(grad_dst, proc_w[layer, 1], NT)
        piece[2] = dot(edge_pick[:, :block], far_grad[...], TN)
        landed(back_in.at[layer], world - 1, recv_sem.at[at_back + layer])
        piece[3] = dot(halo_pick, back_in[layer].reshape(halo, width))
        grad_src = (piece[zero + 2] + piece[zero + 3]).astype(BF16)
        piece[4] = dot(grad_src, proc_w[layer, 0], NT)
        grad = grad + piece[zero] + piece[zero + 1] + piece[zero + 4]

    grad_pre = (grad * slope_of(mesh_pre, mesh_sig)).astype(BF16)
    for c in range(chunks):
        cols = slice(c * part, (c + 1) * part)
        gath_out[c] = dot(grad_pre, mesh_w[cols, :], NT).astype(BF16)
        for off in range(1, sects):
            peer = lax.rem(sect + off, sects)
            push(gath_out.at[c], gath_in.at[c, sect], at_gath + c, (peer, node))
        gath_in[c, sect] = gath_out[c]
    for c in range(chunks):
        landed(gath_in.at[c], sects - 1, recv_sem.at[at_gath + c])
        rows = dot(scat[...], gath_in[c].reshape(whole, part), TN).astype(BF16)
        slot_out[c] = rows.reshape(nodes, cap, part)
        over_nodes(slot_out.at[c], slot_in.at[c], at_slot + c)
        slot_in[c, node] = slot_out[c, node]
    for c in range(chunks):
        cols = slice(c * part, (c + 1) * part)
        landed(slot_in.at[c], nodes - 1, recv_sem.at[at_slot + c])
        back = dot(pick[...], slot_in[c].reshape(slots, part), TN)
        grad_act = jnp.zeros((grid_rows, part), F32)
        for k in range(fanout):
            grad_act = grad_act + (
                back[k * grid_rows : (k + 1) * grid_rows] * act_slope[k, :, cols]
            )
        last_part[c] = dot(grad_act.astype(BF16), enc_w[:, cols], NT)
    total = last_part[zero]
    for c in range(1, chunks):
        total = total + last_part[zero + c]
    grid_grad[...] = total.astype(BF16)

    landed(dst_out, nodes - 1, send_sem.at[at_dst])
    for c in range(chunks):
        landed(msg_out.at[c], nodes - 1, send_sem.at[at_msg + c])
        landed(part_out.at[c], sects - 1, send_sem.at[at_part + c])
        landed(gath_in.at[c], sects - 1, send_sem.at[at_gath + c])
        landed(slot_out.at[c], nodes - 1, send_sem.at[at_slot + c])
    for layer in range(layers):
        landed(halo_out.at[layer], world - 1, send_sem.at[at_halo + layer])
        landed(back_out.at[layer], world - 1, send_sem.at[at_back + layer])


def body(
    grid_feat,
    edge_len,
    g2m_owner,
    g2m_dst,
    enc_weight,
    enc_vec,
    mesh_init,
    mesh_weight,
    halo_send,
    mesh_src,
    proc_weight,
    cot,
):
    nodes = lax.axis_size("node")
    sects = lax.axis_size("sect")
    world = nodes * sects
    grid_rows, width = grid_feat.shape
    fanout = edge_len.shape[1]
    cap = max(2, 2 * grid_rows * fanout // nodes)
    block = mesh_init.shape[1]
    fan = halo_send.shape[4]
    layers = proc_weight.shape[0]
    degree = mesh_src.shape[2]
    slots = nodes * cap
    chunks = CHUNKS
    part = width // chunks
    whole = block * sects
    count = 1 + 4 * chunks + 2 * layers
    vmem = pl.BlockSpec(memory_space=pltpu.VMEM)
    out = pl.pallas_call(
        functools.partial(fused, sects, nodes),
        out_shape=(
            jax.ShapeDtypeStruct((block, width), BF16),
            jax.ShapeDtypeStruct((grid_rows, width), BF16),
        ),
        in_specs=[vmem] * 12,
        out_specs=(vmem, vmem),
        scratch_shapes=[
            pltpu.VMEM((nodes, 1, LANES), F32),
            pltpu.VMEM((nodes, 1, LANES), F32),
            pltpu.VMEM((chunks, nodes, cap, part), BF16),
            pltpu.VMEM((chunks, nodes, cap, part), BF16),
            pltpu.VMEM((chunks, sects, block, part), BF16),
            pltpu.VMEM((chunks, sects, block, part), BF16),
            pltpu.VMEM((layers, world, fan, width), BF16),
            pltpu.VMEM((layers, world, fan, width), BF16),
            pltpu.VMEM((layers, world, fan, width), BF16),
            pltpu.VMEM((layers, world, fan, width), BF16),
            pltpu.VMEM((chunks, block, part), BF16),
            pltpu.VMEM((chunks, sects, block, part), BF16),
            pltpu.VMEM((chunks, nodes, cap, part), BF16),
            pltpu.VMEM((chunks, nodes, cap, part), BF16),
            pltpu.VMEM((slots, fanout * grid_rows), BF16),
            pltpu.VMEM((whole, slots), BF16),
            pltpu.VMEM((degree * block, block + world * fan), BF16),
            pltpu.VMEM((fanout, grid_rows, width), F32),
            pltpu.VMEM((layers, degree * block, width), F32),
            pltpu.VMEM((degree * block, width), F32),
            pltpu.VMEM((degree * block, width), BF16),
            pltpu.VMEM((5, block, width), F32),
            pltpu.VMEM((chunks, grid_rows, width), F32),
            pltpu.SemaphoreType.DMA((count,)),
            pltpu.SemaphoreType.DMA((count,)),
        ],
        compiler_params=pltpu.CompilerParams(
            collective_id=0, has_side_effects=True, vmem_limit_bytes=60 * 2**20
        ),
        name="grid_mesh",
    )(
        grid_feat,
        edge_len,
        g2m_owner.T,
        g2m_dst.T,
        enc_weight,
        enc_vec.reshape(1, width),
        mesh_init[0],
        mesh_weight,
        halo_send.reshape(1, world * fan),
        mesh_src[0],
        proc_weight,
        cot[0],
    )
    return (out[0][None], out[1])


def solution(mesh):
    return jax.shard_map(
        body,
        mesh=mesh,
        in_specs=(
            P(("sect", "node"), None),
            P(("sect", "node"), None),
            P(("sect", "node"), None),
            P(("sect", "node"), None),
            P(),
            P(),
            P("node", "sect", None),
            P(),
            P("sect", "node", None, None, None),
            P("node", "sect", None),
            P(),
            P("node", "sect", None),
        ),
        out_specs=(P("node", "sect", None), P(("sect", "node"), None)),
        check_vma=False,
    )
```

```python
import functools

import jax
import jax.numpy as jnp
from jax import lax
from jax.experimental import pallas as pl
from jax.experimental.pallas import tpu as pltpu
from jax.sharding import PartitionSpec as P

MESH = pl.DeviceIdType.MESH
F32 = jnp.float32
BF16 = jnp.bfloat16
NN = ((1,), (0,))
NT = ((1,), (1,))
TN = ((0,), (0,))
LANES = 128
CHUNKS = 4


def dot(left, right, dims=NN):
    return lax.dot_general(left, right, (dims, ((), ())), preferred_element_type=F32)


def iota(shape, dim):
    return lax.broadcasted_iota(jnp.int32, shape, dim)


def slope_of(value, sig):
    return sig * (1.0 + value * (1.0 - sig))


def fused(
    sects,
    nodes,
    feat,
    length,
    owner,
    dest,
    enc_w,
    vec,
    init,
    mesh_hbm,
    sends,
    sources,
    proc_hbm,
    cot,
    mesh_out,
    grid_grad,
    dst_out,
    dst_in,
    msg_out,
    msg_in,
    part_out,
    part_in,
    halo_out,
    halo_in,
    back_out,
    back_in,
    gath_out,
    gath_in,
    slot_out,
    slot_in,
    pick,
    scat,
    edge_pick,
    act_slope,
    joined,
    far_part,
    mesh_w,
    proc_w,
    load_sem,
    far_grad,
    piece,
    last_part,
    send_sem,
    recv_sem,
):
    sect = lax.axis_index("sect")
    node = lax.axis_index("node")
    world = sects * nodes
    zero = lax.div(sect, sects)
    line = sect * nodes + node
    fanout, grid_rows = length.shape
    degree, block = sources.shape
    width = feat.shape[1]
    whole = block * sects
    cap = msg_out.shape[2]
    slots = nodes * cap
    chunks = msg_out.shape[0]
    part = width // chunks
    layers = proc_w.shape[0]
    fan = halo_out.shape[2]
    halo = world * fan

    loads = [
        pltpu.make_async_copy(mesh_hbm, mesh_w, load_sem.at[0]),
        pltpu.make_async_copy(proc_hbm, proc_w, load_sem.at[1]),
    ]
    for load in loads:
        load.start()

    barrier = pltpu.get_barrier_semaphore()

    def greet_node(step, carry):
        peer = lax.rem(node + step, nodes)
        pl.semaphore_signal(barrier, inc=1, device_id=(sect, peer), device_id_type=MESH)
        return carry

    def greet_sect(step, carry):
        peer = lax.rem(sect + step, sects)
        pl.semaphore_signal(barrier, inc=1, device_id=(peer, node), device_id_type=MESH)
        return carry

    lax.fori_loop(1, nodes, greet_node, 0)
    lax.fori_loop(1, sects, greet_sect, 0)

    def push(src, dst, at, device):
        pltpu.make_async_remote_copy(
            src_ref=src,
            dst_ref=dst,
            send_sem=send_sem.at[at],
            recv_sem=recv_sem.at[at],
            device_id=device,
            device_id_type=MESH,
        ).start()

    def over_nodes(src, dst, at):
        def step(off, carry):
            peer = lax.rem(node + off, nodes)
            push(src.at[peer], dst.at[node], at, (sect, peer))
            return carry

        lax.fori_loop(1, nodes, step, 0, unroll=9)

    def over_all(src, dst, at):
        def step(off, carry):
            peer = lax.rem(line + off, world)
            push(
                src.at[peer],
                dst.at[line],
                at,
                (lax.div(peer, nodes), lax.rem(peer, nodes)),
            )
            return carry

        lax.fori_loop(1, world, step, 0, unroll=15)

    def landed(ref, count, sem):
        some = ref.at[pl.ds(0, count)]
        pltpu.make_async_copy(some, some, sem).wait()

    at_dst = 0
    at_msg = 1
    at_part = at_msg + chunks
    at_halo = at_part + chunks
    at_back = at_halo + layers
    at_gath = at_back + layers
    at_slot = at_gath + chunks

    upper = (iota((grid_rows, grid_rows), 0) < iota((grid_rows, grid_rows), 1)).astype(BF16)
    used = jnp.zeros((nodes, 1), F32)
    table = jnp.zeros((nodes, LANES), F32)
    for k in range(fanout):
        own_row = owner[k : k + 1, :]
        dst_row = dest[k : k + 1, :]
        hot = (iota((nodes, grid_rows), 0) == own_row).astype(F32)
        before = dot(hot.astype(BF16), upper) + used
        rank = jnp.sum(hot * before, axis=0, keepdims=True).astype(jnp.int32)
        used = used + jnp.sum(hot, axis=1, keepdims=True)
        place = own_row * cap + rank
        pick[:, k * grid_rows : (k + 1) * grid_rows] = (
            iota((slots, grid_rows), 0) == place
        ).astype(BF16)
        level = (iota((LANES, grid_rows), 0) == rank).astype(BF16)
        high = (hot * (dst_row >> 4).astype(F32)).astype(BF16)
        low = (hot * ((dst_row & 15) + 1).astype(F32)).astype(BF16)
        table = table + 16.0 * dot(high, level, NT) + dot(low, level, NT)
    dst_out[...] = table.reshape(nodes, 1, LANES)

    pre = dot(feat[...], enc_w[...])
    acts = []
    for k in range(fanout):
        column = jnp.broadcast_to(length[k : k + 1, :], (8, grid_rows)).T[:, 0:1]
        acts.append(pre + column * vec[...])
    sigs = [jax.nn.sigmoid(act) for act in acts]
    message = jnp.concatenate(
        [(act * sig).astype(BF16) for act, sig in zip(acts, sigs)], axis=0
    )

    pl.semaphore_wait(barrier, nodes + sects - 2)
    over_nodes(dst_out, dst_in, at_dst)
    dst_in[node] = dst_out[node]
    for c in range(chunks):
        cols = slice(c * part, (c + 1) * part)
        msg_out[c] = dot(pick[...], message[:, cols]).astype(BF16).reshape(nodes, cap, part)
        over_nodes(msg_out.at[c], msg_in.at[c], at_msg + c)
        msg_in[c, node] = msg_out[c, node]

    for k in range(fanout):
        act_slope[k] = slope_of(acts[k], sigs[k])

    for k in range(degree):
        edge_pick[:, k * block : (k + 1) * block] = (
            iota((block + halo, block), 0) == sources[k : k + 1, :]
        ).astype(BF16)
    order = iota((nodes, halo), 1)
    spread = (lax.rem(lax.div(order, fan), nodes) == iota((nodes, halo), 0)).astype(BF16)
    order = iota((sects * fan, halo), 1)
    mine = lax.div(order, fan * nodes) * fan + lax.rem(order, fan) == iota(order.shape, 0)
    wide = dot(sends[...].astype(F32).astype(BF16), spread)
    sent = jnp.sum(jnp.where(mine, wide, 0.0), axis=0, keepdims=True).astype(jnp.int32)
    halo_pick = (iota((block, halo), 0) == sent).astype(BF16)

    landed(dst_in, nodes - 1, recv_sem.at[at_dst])
    got = dst_in[...].reshape(nodes, LANES)
    got_high = jnp.floor(got * (1.0 / 16.0))
    got_low = got - 16.0 * got_high
    spread = (lax.rem(iota((LANES, slots), 1), cap) == iota((LANES, slots), 0)).astype(BF16)
    mine = (lax.div(iota((nodes, slots), 1), cap) == iota((nodes, slots), 0)).astype(F32)
    wide = 16.0 * dot(got_high.astype(BF16), spread) + dot(got_low.astype(BF16), spread)
    got_row = jnp.sum(wide * mine, axis=0, keepdims=True).astype(jnp.int32) - 1
    scat[...] = (iota((whole, slots), 0) == got_row).astype(BF16)

    mesh_pre = jnp.zeros((block, width), F32)
    for load in loads:
        load.wait()
    for c in range(chunks):
        landed(msg_in.at[c], nodes - 1, recv_sem.at[at_msg + c])
        agg = dot(scat[...], msg_in[c].reshape(slots, part))
        part_out[c] = agg.astype(BF16).reshape(sects, block, part)
        for off in range(1, sects):
            peer = lax.rem(sect + off, sects)
            push(part_out.at[c, peer], part_in.at[c, sect], at_part + c, (peer, node))
        part_in[c, sect] = part_out[c, sect]
    for c in range(chunks):
        landed(part_in.at[c], sects - 1, recv_sem.at[at_part + c])
        total = jnp.sum(part_in[c].astype(F32), axis=0)
        last_part[c, :block, :] = dot(total.astype(BF16), mesh_w[c * part : (c + 1) * part, :])
    for c in range(chunks):
        mesh_pre = mesh_pre + last_part[zero + c, :block, :]
    mesh_sig = jax.nn.sigmoid(mesh_pre)
    state = (init[...].astype(F32) + mesh_pre * mesh_sig).astype(BF16)

    saved = []
    for layer in range(layers):
        out = dot(halo_pick, state, TN).astype(BF16)
        halo_out[layer] = out.reshape(world, fan, width)
        over_all(halo_out.at[layer], halo_in.at[layer], at_halo + layer)
        halo_in[layer, line] = halo_out[layer, line]
        near = dot(edge_pick[:block, :], state, TN).astype(BF16)
        piece[2] = dot(state, proc_w[layer, 1])
        joined[layer] = dot(near, proc_w[layer, 0])
        piece[1] = dot(state, proc_w[layer, 2])
        if layer > 0:
            prev = joined[layer - 1]
            joined[layer - 1] = slope_of(prev, jax.nn.sigmoid(prev))
        landed(halo_in.at[layer], world - 1, recv_sem.at[at_halo + layer])
        far = dot(edge_pick[block:, :], halo_in[layer].reshape(halo, width), TN).astype(BF16)
        far_part[...] = dot(far, proc_w[layer, 0])
        agg = jnp.zeros((block, width), F32)
        to_dst = piece[zero + 2]
        for k in range(degree):
            rows = slice(k * block, (k + 1) * block)
            full = joined[zero + layer, rows, :] + far_part[rows, :] + to_dst
            joined[layer, rows, :] = full
            agg = agg + full * jax.nn.sigmoid(full)
        agg = agg.astype(BF16)
        piece[0] = dot(agg, proc_w[layer, 3])
        mixed = piece[zero + 1] + piece[zero]
        centred = mixed - jnp.mean(mixed, axis=1, keepdims=True)
        scale = lax.rsqrt(jnp.mean(centred * centred, axis=1, keepdims=True) + 1e-05)
        normed = centred * scale
        sig = jax.nn.sigmoid(normed)
        saved.append((normed, scale, slope_of(normed, sig)))
        state = (state.astype(F32) + normed * sig).astype(BF16)
    mesh_out[...] = state
    last = joined[layers - 1]
    joined[layers - 1] = slope_of(last, jax.nn.sigmoid(last))

    grad = cot[...].astype(F32)
    for layer in reversed(range(layers)):
        normed, scale, slope = saved[layer]
        grad_normed = grad * slope
        grad_mixed = scale * (
            grad_normed
            - jnp.mean(grad_normed, axis=1, keepdims=True)
            - normed * jnp.mean(grad_normed * normed, axis=1, keepdims=True)
        )
        grad_mixed = grad_mixed.astype(BF16)
        grad_agg = dot(grad_mixed, proc_w[layer, 3], NT)
        grad_dst = jnp.zeros((block, width), F32)
        for k in range(degree):
            rows = slice(k * block, (k + 1) * block)
            grad_joined = joined[layer, rows, :] * grad_agg
            grad_dst = grad_dst + grad_joined
            far_grad[rows, :] = grad_joined.astype(BF16)
        grad_dst = grad_dst.astype(BF16)
        out = dot(edge_pick[block:, :], far_grad[...]).astype(BF16)
        back_out[layer] = out.reshape(world, fan, width)
        over_all(back_out.at[layer], back_in.at[layer], at_back + layer)
        back_in[layer, line] = back_out[layer, line]
        piece[0] = dot(grad_mixed, proc_w[layer, 2], NT)
        piece[1] = dot(grad_dst, proc_w[layer, 1], NT)
        piece[2] = dot(edge_pick[:block, :], far_grad[...])
        landed(back_in.at[layer], world - 1, recv_sem.at[at_back + layer])
        piece[3] = dot(halo_pick, back_in[layer].reshape(halo, width))
        grad_src = (piece[zero + 2] + piece[zero + 3]).astype(BF16)
        piece[4] = dot(grad_src, proc_w[layer, 0], NT)
        grad = grad + piece[zero] + piece[zero + 1] + piece[zero + 4]

    grad_pre = (grad * slope_of(mesh_pre, mesh_sig)).astype(BF16)
    for c in range(chunks):
        cols = slice(c * part, (c + 1) * part)
        gath_out[c] = dot(grad_pre, mesh_w[cols, :], NT).astype(BF16)
        for off in range(1, sects):
            peer = lax.rem(sect + off, sects)
            push(gath_out.at[c], gath_in.at[c, sect], at_gath + c, (peer, node))
        gath_in[c, sect] = gath_out[c]
    for c in range(chunks):
        landed(gath_in.at[c], sects - 1, recv_sem.at[at_gath + c])
        rows = dot(scat[...], gath_in[c].reshape(whole, part), TN).astype(BF16)
        slot_out[c] = rows.reshape(nodes, cap, part)
        over_nodes(slot_out.at[c], slot_in.at[c], at_slot + c)
        slot_in[c, node] = slot_out[c, node]
    for c in range(chunks):
        cols = slice(c * part, (c + 1) * part)
        landed(slot_in.at[c], nodes - 1, recv_sem.at[at_slot + c])
        back = dot(pick[...], slot_in[c].reshape(slots, part), TN)
        grad_act = jnp.zeros((grid_rows, part), F32)
        for k in range(fanout):
            grad_act = grad_act + (
                back[k * grid_rows : (k + 1) * grid_rows] * act_slope[k, :, cols]
            )
        last_part[c] = dot(grad_act.astype(BF16), enc_w[:, cols], NT)
    total = last_part[zero]
    for c in range(1, chunks):
        total = total + last_part[zero + c]
    grid_grad[...] = total.astype(BF16)

    landed(dst_out, nodes - 1, send_sem.at[at_dst])
    for c in range(chunks):
        landed(msg_out.at[c], nodes - 1, send_sem.at[at_msg + c])
        landed(part_out.at[c], sects - 1, send_sem.at[at_part + c])
        landed(gath_in.at[c], sects - 1, send_sem.at[at_gath + c])
        landed(slot_out.at[c], nodes - 1, send_sem.at[at_slot + c])
    for layer in range(layers):
        landed(halo_out.at[layer], world - 1, send_sem.at[at_halo + layer])
        landed(back_out.at[layer], world - 1, send_sem.at[at_back + layer])


def finish(state, grad, mesh_out, grid_grad):
    mesh_out[...] = state[...]
    grid_grad[...] = grad[...]


def body(
    grid_feat,
    edge_len,
    g2m_owner,
    g2m_dst,
    enc_weight,
    enc_vec,
    mesh_init,
    mesh_weight,
    halo_send,
    mesh_src,
    proc_weight,
    cot,
):
    nodes = lax.axis_size("node")
    sects = lax.axis_size("sect")
    world = nodes * sects
    grid_rows, width = grid_feat.shape
    fanout = edge_len.shape[1]
    cap = max(2, 2 * grid_rows * fanout // nodes)
    block = mesh_init.shape[1]
    fan = halo_send.shape[4]
    layers = proc_weight.shape[0]
    degree = mesh_src.shape[2]
    slots = nodes * cap
    chunks = CHUNKS
    part = width // chunks
    whole = block * sects
    count = 1 + 4 * chunks + 2 * layers
    vmem = pl.BlockSpec(memory_space=pltpu.VMEM)
    hbm = pl.BlockSpec(memory_space=pl.ANY)
    out_shape = (
        jax.ShapeDtypeStruct((block, width), BF16),
        jax.ShapeDtypeStruct((grid_rows, width), BF16),
    )
    out = pl.pallas_call(
        functools.partial(fused, sects, nodes),
        out_shape=out_shape,
        in_specs=[vmem] * 7 + [hbm, vmem, vmem, hbm, vmem],
        out_specs=(vmem, vmem),
        scratch_shapes=[
            pltpu.VMEM((nodes, 1, LANES), F32),
            pltpu.VMEM((nodes, 1, LANES), F32),
            pltpu.VMEM((chunks, nodes, cap, part), BF16),
            pltpu.VMEM((chunks, nodes, cap, part), BF16),
            pltpu.VMEM((chunks, sects, block, part), BF16),
            pltpu.VMEM((chunks, sects, block, part), BF16),
            pltpu.VMEM((layers, world, fan, width), BF16),
            pltpu.VMEM((layers, world, fan, width), BF16),
            pltpu.VMEM((layers, world, fan, width), BF16),
            pltpu.VMEM((layers, world, fan, width), BF16),
            pltpu.VMEM((chunks, block, part), BF16),
            pltpu.VMEM((chunks, sects, block, part), BF16),
            pltpu.VMEM((chunks, nodes, cap, part), BF16),
            pltpu.VMEM((chunks, nodes, cap, part), BF16),
            pltpu.VMEM((slots, fanout * grid_rows), BF16),
            pltpu.VMEM((whole, slots), BF16),
            pltpu.VMEM((block + world * fan, degree * block), BF16),
            pltpu.VMEM((fanout, grid_rows, width), F32),
            pltpu.VMEM((layers, degree * block, width), F32),
            pltpu.VMEM((degree * block, width), F32),
            pltpu.VMEM(mesh_weight.shape, BF16),
            pltpu.VMEM(proc_weight.shape, BF16),
            pltpu.SemaphoreType.DMA((2,)),
            pltpu.VMEM((degree * block, width), BF16),
            pltpu.VMEM((5, block, width), F32),
            pltpu.VMEM((chunks, grid_rows, width), F32),
            pltpu.SemaphoreType.DMA((count,)),
            pltpu.SemaphoreType.DMA((count,)),
        ],
        compiler_params=pltpu.CompilerParams(
            collective_id=0, has_side_effects=True, vmem_limit_bytes=60 * 2**20
        ),
        name="grid_mesh",
    )(
        grid_feat,
        edge_len.T,
        g2m_owner.T,
        g2m_dst.T,
        enc_weight,
        enc_vec.reshape(1, width),
        mesh_init[0],
        mesh_weight,
        halo_send[0, 0].transpose(0, 2, 1).reshape(sects * fan, nodes),
        mesh_src[0].T,
        proc_weight,
        cot[0],
    )
    out = pl.pallas_call(
        finish,
        out_shape=out_shape,
        in_specs=[vmem] * 2,
        out_specs=(vmem, vmem),
        name="finish",
    )(*out)
    return (out[0][None], out[1])


def solution(mesh):
    return jax.shard_map(
        body,
        mesh=mesh,
        in_specs=(
            P(("sect", "node"), None),
            P(("sect", "node"), None),
            P(("sect", "node"), None),
            P(("sect", "node"), None),
            P(),
            P(),
            P("node", "sect", None),
            P(),
            P("sect", "node", None, None, None),
            P("node", "sect", None),
            P(),
            P("node", "sect", None),
        ),
        out_specs=(P("node", "sect", None), P(("sect", "node"), None)),
        check_vma=False,
    )
```

```python
import functools

import jax
import jax.numpy as jnp
from jax import lax
from jax.experimental import pallas as pl
from jax.experimental.pallas import tpu as pltpu
from jax.sharding import PartitionSpec as P

MESH = pl.DeviceIdType.MESH
F32 = jnp.float32
BF16 = jnp.bfloat16
NN = ((1,), (0,))
NT = ((1,), (1,))
TN = ((0,), (0,))
LANES = 128
CHUNKS = 4


def dot(left, right, dims=NN):
    return lax.dot_general(left, right, (dims, ((), ())), preferred_element_type=F32)


def iota(shape, dim):
    return lax.broadcasted_iota(jnp.int32, shape, dim)


def slope_of(value, sig):
    return sig * (1.0 + value * (1.0 - sig))


def fused(
    sects,
    nodes,
    feat_hbm,
    length,
    owner,
    dest,
    enc_hbm,
    vec,
    init,
    mesh_hbm,
    sends,
    sources,
    proc_hbm,
    cot,
    mesh_out,
    grid_grad,
    dst_out,
    dst_in,
    msg_out,
    msg_in,
    part_out,
    part_in,
    halo_out,
    halo_in,
    back_out,
    back_in,
    gath_out,
    gath_in,
    slot_out,
    slot_in,
    pick,
    scat,
    edge_pick,
    halo_pick,
    act_slope,
    joined,
    far_part,
    feat,
    enc_w,
    mesh_w,
    proc_w,
    load_sem,
    far_grad,
    piece,
    last_part,
    send_sem,
    recv_sem,
):
    sect = lax.axis_index("sect")
    node = lax.axis_index("node")
    world = sects * nodes
    zero = lax.div(sect, sects)
    line = sect * nodes + node
    fanout, grid_rows = length.shape
    degree, block = sources.shape
    width = feat.shape[1]
    whole = block * sects
    cap = msg_out.shape[2]
    slots = nodes * cap
    chunks = msg_out.shape[0]
    part = width // chunks
    layers = proc_w.shape[0]
    fan = halo_out.shape[2]
    halo = world * fan
    span = nodes * fan

    loads = [
        pltpu.make_async_copy(feat_hbm, feat, load_sem.at[0]),
        pltpu.make_async_copy(enc_hbm, enc_w, load_sem.at[1]),
        pltpu.make_async_copy(mesh_hbm, mesh_w, load_sem.at[2]),
        pltpu.make_async_copy(proc_hbm, proc_w, load_sem.at[3]),
    ]
    for load in loads:
        load.start()

    barrier = pltpu.get_barrier_semaphore()

    def greet_node(step, carry):
        peer = lax.rem(node + step, nodes)
        pl.semaphore_signal(barrier, inc=1, device_id=(sect, peer), device_id_type=MESH)
        return carry

    def greet_sect(step, carry):
        peer = lax.rem(sect + step, sects)
        pl.semaphore_signal(barrier, inc=1, device_id=(peer, node), device_id_type=MESH)
        return carry

    lax.fori_loop(1, nodes, greet_node, 0)
    lax.fori_loop(1, sects, greet_sect, 0)

    def push(src, dst, at, device):
        pltpu.make_async_remote_copy(
            src_ref=src,
            dst_ref=dst,
            send_sem=send_sem.at[at],
            recv_sem=recv_sem.at[at],
            device_id=device,
            device_id_type=MESH,
        ).start()

    def over_nodes(src, dst, at):
        def step(off, carry):
            peer = lax.rem(node + off, nodes)
            push(src.at[peer], dst.at[node], at, (sect, peer))
            return carry

        lax.fori_loop(1, nodes, step, 0, unroll=9)

    def over_sect(src, dst, at, peer_sect, first):
        def step(off, carry):
            peer = lax.rem(node + off, nodes)
            push(src.at[peer_sect * nodes + peer], dst.at[line], at, (peer_sect, peer))
            return carry

        lax.fori_loop(int(first), nodes, step, 0, unroll=9 if first else 8)

    def landed(ref, count, sem):
        some = ref.at[pl.ds(0, count)]
        pltpu.make_async_copy(some, some, sem).wait()

    at_dst = 0
    at_msg = 1
    at_part = at_msg + chunks
    at_halo = at_part + chunks
    at_back = at_halo + layers
    at_gath = at_back + layers
    at_slot = at_gath + chunks

    upper = (iota((grid_rows, grid_rows), 0) < iota((grid_rows, grid_rows), 1)).astype(BF16)
    used = jnp.zeros((nodes, 1), F32)
    hots, ranks, columns = [], [], []
    for k in range(fanout):
        own_row = owner[k : k + 1, :]
        hot = (iota((nodes, grid_rows), 0) == own_row).astype(F32)
        before = dot(hot.astype(BF16), upper) + used
        rank = jnp.sum(hot * before, axis=0, keepdims=True).astype(jnp.int32)
        used = used + jnp.sum(hot, axis=1, keepdims=True)
        place = own_row * cap + rank
        pick[:, k * grid_rows : (k + 1) * grid_rows] = (
            iota((slots, grid_rows), 0) == place
        ).astype(BF16)
        hots.append(hot)
        ranks.append(rank)
        columns.append(jnp.broadcast_to(length[k : k + 1, :], (8, grid_rows)).T[:, 0:1])

    for load in loads[:2]:
        load.wait()
    for c in range(chunks):
        cols = slice(c * part, (c + 1) * part)
        pre = dot(feat[...], enc_w[:, cols])
        message = []
        for k in range(fanout):
            act = pre + columns[k] * vec[:, cols]
            sig = jax.nn.sigmoid(act)
            message.append((act * sig).astype(BF16))
            act_slope[k, :, cols] = slope_of(act, sig)
        message = jnp.concatenate(message, axis=0)
        msg_out[c] = dot(pick[...], message).astype(BF16).reshape(nodes, cap, part)
        if c == 0:
            pl.semaphore_wait(barrier, nodes + sects - 2)
        over_nodes(msg_out.at[c], msg_in.at[c], at_msg + c)
        msg_in[c, node] = msg_out[c, node]
        if c == 0:
            table = jnp.zeros((nodes, LANES), F32)
            for k in range(fanout):
                dst_row = dest[k : k + 1, :]
                level = (iota((LANES, grid_rows), 0) == ranks[k]).astype(BF16)
                high = (hots[k] * (dst_row >> 4).astype(F32)).astype(BF16)
                low = (hots[k] * ((dst_row & 15) + 1).astype(F32)).astype(BF16)
                table = table + 16.0 * dot(high, level, NT) + dot(low, level, NT)
            dst_out[...] = table.reshape(nodes, 1, LANES)
            over_nodes(dst_out, dst_in, at_dst)
            dst_in[node] = dst_out[node]

    for k in range(degree):
        edge_pick[:, k * block : (k + 1) * block] = (
            iota((block + halo, block), 0) == sources[k : k + 1, :]
        ).astype(BF16)
    order = iota((nodes, halo), 1)
    spread = (lax.rem(lax.div(order, fan), nodes) == iota((nodes, halo), 0)).astype(BF16)
    order = iota((sects * fan, halo), 1)
    mine = lax.div(order, fan * nodes) * fan + lax.rem(order, fan) == iota(order.shape, 0)
    wide = dot(sends[...].astype(F32).astype(BF16), spread)
    sent = jnp.sum(jnp.where(mine, wide, 0.0), axis=0, keepdims=True).astype(jnp.int32)
    halo_pick[...] = (iota((block, halo), 0) == sent).astype(BF16)

    landed(dst_in, nodes - 1, recv_sem.at[at_dst])
    got = dst_in[...].reshape(nodes, LANES)
    got_high = jnp.floor(got * (1.0 / 16.0))
    got_low = got - 16.0 * got_high
    spread = (lax.rem(iota((LANES, slots), 1), cap) == iota((LANES, slots), 0)).astype(BF16)
    mine = (lax.div(iota((nodes, slots), 1), cap) == iota((nodes, slots), 0)).astype(F32)
    wide = 16.0 * dot(got_high.astype(BF16), spread) + dot(got_low.astype(BF16), spread)
    got_row = jnp.sum(wide * mine, axis=0, keepdims=True).astype(jnp.int32) - 1
    scat[...] = (iota((whole, slots), 0) == got_row).astype(BF16)

    mesh_pre = jnp.zeros((block, width), F32)
    for load in loads[2:]:
        load.wait()
    for c in range(chunks):
        landed(msg_in.at[c], nodes - 1, recv_sem.at[at_msg + c])
        agg = dot(scat[...], msg_in[c].reshape(slots, part))
        part_out[c] = agg.astype(BF16).reshape(sects, block, part)
        for off in range(1, sects):
            peer = lax.rem(sect + off, sects)
            push(part_out.at[c, peer], part_in.at[c, sect], at_part + c, (peer, node))
        part_in[c, sect] = part_out[c, sect]
    for c in range(chunks):
        landed(part_in.at[c], sects - 1, recv_sem.at[at_part + c])
        total = jnp.sum(part_in[c].astype(F32), axis=0)
        last_part[c, :block, :] = dot(total.astype(BF16), mesh_w[c * part : (c + 1) * part, :])
    for c in range(chunks):
        mesh_pre = mesh_pre + last_part[zero + c, :block, :]
    mesh_sig = jax.nn.sigmoid(mesh_pre)
    state = (init[...].astype(F32) + mesh_pre * mesh_sig).astype(BF16)

    saved = []
    for layer in range(layers):
        for off in range(sects):
            peer = lax.rem(sect + off, sects)
            cols = pl.ds(pl.multiple_of(peer * span, span), span)
            out = dot(halo_pick[:, cols], state, TN).astype(BF16)
            halo_out[layer, pl.ds(peer * nodes, nodes)] = out.reshape(nodes, fan, width)
            over_sect(halo_out.at[layer], halo_in.at[layer], at_halo + layer, peer, off == 0)
        halo_in[layer, line] = halo_out[layer, line]
        near = dot(edge_pick[:block, :], state, TN).astype(BF16)
        piece[2] = dot(state, proc_w[layer, 1])
        joined[layer] = dot(near, proc_w[layer, 0])
        piece[1] = dot(state, proc_w[layer, 2])
        if layer > 0:
            prev = joined[layer - 1]
            joined[layer - 1] = slope_of(prev, jax.nn.sigmoid(prev))
        landed(halo_in.at[layer], world - 1, recv_sem.at[at_halo + layer])
        incoming = halo_in[layer].reshape(halo, width)
        agg = jnp.zeros((block, width), F32)
        to_dst = piece[zero + 2]
        for k in range(degree):
            if k % (degree // 2) == 0:
                some = slice(k * block, (k + degree // 2) * block)
                far = dot(edge_pick[block:, some], incoming, TN).astype(BF16)
                far_part[some, :] = dot(far, proc_w[layer, 0])
            rows = slice(k * block, (k + 1) * block)
            full = joined[zero + layer, rows, :] + far_part[rows, :] + to_dst
            gate = jax.nn.sigmoid(full)
            joined[layer, rows, :] = full if layer < layers - 1 else slope_of(full, gate)
            agg = agg + full * gate
        agg = agg.astype(BF16)
        piece[0] = dot(agg, proc_w[layer, 3])
        mixed = piece[zero + 1] + piece[zero]
        centred = mixed - jnp.mean(mixed, axis=1, keepdims=True)
        scale = lax.rsqrt(jnp.mean(centred * centred, axis=1, keepdims=True) + 1e-05)
        normed = centred * scale
        sig = jax.nn.sigmoid(normed)
        saved.append((normed, scale, slope_of(normed, sig)))
        state = (state.astype(F32) + normed * sig).astype(BF16)
    mesh_out[...] = state

    grad = cot[...].astype(F32)
    for layer in reversed(range(layers)):
        normed, scale, slope = saved[layer]
        grad_normed = grad * slope
        grad_mixed = scale * (
            grad_normed
            - jnp.mean(grad_normed, axis=1, keepdims=True)
            - normed * jnp.mean(grad_normed * normed, axis=1, keepdims=True)
        )
        grad_mixed = grad_mixed.astype(BF16)
        grad_agg = dot(grad_mixed, proc_w[layer, 3], NT)
        grad_dst = jnp.zeros((block, width), F32)
        for k in range(degree):
            rows = slice(k * block, (k + 1) * block)
            grad_joined = joined[layer, rows, :] * grad_agg
            grad_dst = grad_dst + grad_joined
            far_grad[rows, :] = grad_joined.astype(BF16)
        grad_dst = grad_dst.astype(BF16)
        for off in range(sects):
            peer = lax.rem(sect + off, sects)
            rows = pl.ds(pl.multiple_of(block + peer * span, span), span)
            out = dot(edge_pick[rows, :], far_grad[...]).astype(BF16)
            back_out[layer, pl.ds(peer * nodes, nodes)] = out.reshape(nodes, fan, width)
            over_sect(back_out.at[layer], back_in.at[layer], at_back + layer, peer, off == 0)
        back_in[layer, line] = back_out[layer, line]
        piece[0] = dot(grad_mixed, proc_w[layer, 2], NT)
        piece[1] = dot(grad_dst, proc_w[layer, 1], NT)
        piece[2] = dot(edge_pick[:block, :], far_grad[...])
        landed(back_in.at[layer], world - 1, recv_sem.at[at_back + layer])
        piece[3] = dot(halo_pick[...], back_in[layer].reshape(halo, width))
        grad_src = (piece[zero + 2] + piece[zero + 3]).astype(BF16)
        piece[4] = dot(grad_src, proc_w[layer, 0], NT)
        grad = grad + piece[zero] + piece[zero + 1] + piece[zero + 4]

    grad_pre = (grad * slope_of(mesh_pre, mesh_sig)).astype(BF16)
    for c in range(chunks):
        cols = slice(c * part, (c + 1) * part)
        gath_out[c] = dot(grad_pre, mesh_w[cols, :], NT).astype(BF16)
        for off in range(1, sects):
            peer = lax.rem(sect + off, sects)
            push(gath_out.at[c], gath_in.at[c, sect], at_gath + c, (peer, node))
        gath_in[c, sect] = gath_out[c]
    for c in range(chunks):
        landed(gath_in.at[c], sects - 1, recv_sem.at[at_gath + c])
        rows = dot(scat[...], gath_in[c].reshape(whole, part), TN).astype(BF16)
        slot_out[c] = rows.reshape(nodes, cap, part)
        over_nodes(slot_out.at[c], slot_in.at[c], at_slot + c)
        slot_in[c, node] = slot_out[c, node]
    for c in range(chunks):
        cols = slice(c * part, (c + 1) * part)
        landed(slot_in.at[c], nodes - 1, recv_sem.at[at_slot + c])
        back = dot(pick[...], slot_in[c].reshape(slots, part), TN)
        grad_act = jnp.zeros((grid_rows, part), F32)
        for k in range(fanout):
            grad_act = grad_act + (
                back[k * grid_rows : (k + 1) * grid_rows] * act_slope[k, :, cols]
            )
        last_part[c] = dot(grad_act.astype(BF16), enc_w[:, cols], NT)
    total = last_part[zero]
    for c in range(1, chunks):
        total = total + last_part[zero + c]
    grid_grad[...] = total.astype(BF16)

    landed(dst_out, nodes - 1, send_sem.at[at_dst])
    for c in range(chunks):
        landed(msg_out.at[c], nodes - 1, send_sem.at[at_msg + c])
        landed(part_out.at[c], sects - 1, send_sem.at[at_part + c])
        landed(gath_in.at[c], sects - 1, send_sem.at[at_gath + c])
        landed(slot_out.at[c], nodes - 1, send_sem.at[at_slot + c])
    for layer in range(layers):
        landed(halo_out.at[layer], world - 1, send_sem.at[at_halo + layer])
        landed(back_out.at[layer], world - 1, send_sem.at[at_back + layer])


def finish(state, grad, mesh_out, grid_grad):
    mesh_out[...] = state[...]
    grid_grad[...] = grad[...]


def body(
    grid_feat,
    edge_len,
    g2m_owner,
    g2m_dst,
    enc_weight,
    enc_vec,
    mesh_init,
    mesh_weight,
    halo_send,
    mesh_src,
    proc_weight,
    cot,
):
    nodes = lax.axis_size("node")
    sects = lax.axis_size("sect")
    world = nodes * sects
    grid_rows, width = grid_feat.shape
    fanout = edge_len.shape[1]
    cap = max(2, 2 * grid_rows * fanout // nodes)
    block = mesh_init.shape[1]
    fan = halo_send.shape[4]
    layers = proc_weight.shape[0]
    degree = mesh_src.shape[2]
    slots = nodes * cap
    chunks = CHUNKS
    part = width // chunks
    whole = block * sects
    count = 1 + 4 * chunks + 2 * layers
    vmem = pl.BlockSpec(memory_space=pltpu.VMEM)
    hbm = pl.BlockSpec(memory_space=pl.ANY)
    out_shape = (
        jax.ShapeDtypeStruct((block, width), BF16),
        jax.ShapeDtypeStruct((grid_rows, width), BF16),
    )
    out = pl.pallas_call(
        functools.partial(fused, sects, nodes),
        out_shape=out_shape,
        in_specs=[hbm, vmem, vmem, vmem, hbm, vmem, vmem, hbm, vmem, vmem, hbm, vmem],
        out_specs=(vmem, vmem),
        scratch_shapes=[
            pltpu.VMEM((nodes, 1, LANES), F32),
            pltpu.VMEM((nodes, 1, LANES), F32),
            pltpu.VMEM((chunks, nodes, cap, part), BF16),
            pltpu.VMEM((chunks, nodes, cap, part), BF16),
            pltpu.VMEM((chunks, sects, block, part), BF16),
            pltpu.VMEM((chunks, sects, block, part), BF16),
            pltpu.VMEM((layers, world, fan, width), BF16),
            pltpu.VMEM((layers, world, fan, width), BF16),
            pltpu.VMEM((layers, world, fan, width), BF16),
            pltpu.VMEM((layers, world, fan, width), BF16),
            pltpu.VMEM((chunks, block, part), BF16),
            pltpu.VMEM((chunks, sects, block, part), BF16),
            pltpu.VMEM((chunks, nodes, cap, part), BF16),
            pltpu.VMEM((chunks, nodes, cap, part), BF16),
            pltpu.VMEM((slots, fanout * grid_rows), BF16),
            pltpu.VMEM((whole, slots), BF16),
            pltpu.VMEM((block + world * fan, degree * block), BF16),
            pltpu.VMEM((block, world * fan), BF16),
            pltpu.VMEM((fanout, grid_rows, width), F32),
            pltpu.VMEM((layers, degree * block, width), F32),
            pltpu.VMEM((degree * block, width), F32),
            pltpu.VMEM(grid_feat.shape, BF16),
            pltpu.VMEM(enc_weight.shape, BF16),
            pltpu.VMEM(mesh_weight.shape, BF16),
            pltpu.VMEM(proc_weight.shape, BF16),
            pltpu.SemaphoreType.DMA((4,)),
            pltpu.VMEM((degree * block, width), BF16),
            pltpu.VMEM((5, block, width), F32),
            pltpu.VMEM((chunks, grid_rows, width), F32),
            pltpu.SemaphoreType.DMA((count,)),
            pltpu.SemaphoreType.DMA((count,)),
        ],
        compiler_params=pltpu.CompilerParams(
            collective_id=0, has_side_effects=True, vmem_limit_bytes=60 * 2**20
        ),
        name="grid_mesh",
    )(
        grid_feat,
        edge_len.T,
        g2m_owner.T,
        g2m_dst.T,
        enc_weight,
        enc_vec.reshape(1, width),
        mesh_init[0],
        mesh_weight,
        halo_send[0, 0].transpose(0, 2, 1).reshape(sects * fan, nodes),
        mesh_src[0].T,
        proc_weight,
        cot[0],
    )
    out = pl.pallas_call(
        finish,
        out_shape=out_shape,
        in_specs=[vmem] * 2,
        out_specs=(vmem, vmem),
        name="finish",
    )(*out)
    return (out[0][None], out[1])


def solution(mesh):
    return jax.shard_map(
        body,
        mesh=mesh,
        in_specs=(
            P(("sect", "node"), None),
            P(("sect", "node"), None),
            P(("sect", "node"), None),
            P(("sect", "node"), None),
            P(),
            P(),
            P("node", "sect", None),
            P(),
            P("sect", "node", None, None, None),
            P("node", "sect", None),
            P(),
            P("node", "sect", None),
        ),
        out_specs=(P("node", "sect", None), P(("sect", "node"), None)),
        check_vma=False,
    )
```

```python
import functools

import jax
import jax.numpy as jnp
from jax import lax
from jax.experimental import pallas as pl
from jax.experimental.pallas import tpu as pltpu
from jax.sharding import PartitionSpec as P

MESH = pl.DeviceIdType.MESH
F32 = jnp.float32
BF16 = jnp.bfloat16
NN = ((1,), (0,))
NT = ((1,), (1,))
TN = ((0,), (0,))
LANES = 128
CHUNKS = 4


def dot(left, right, dims=NN):
    return lax.dot_general(left, right, (dims, ((), ())), preferred_element_type=F32)


def iota(shape, dim):
    return lax.broadcasted_iota(jnp.int32, shape, dim)


def slope_of(value, sig):
    return sig * (1.0 + value * (1.0 - sig))


def fused(
    sects,
    nodes,
    feat_hbm,
    length,
    owner,
    dest,
    enc_hbm,
    vec,
    init,
    mesh_hbm,
    sends,
    sources,
    proc_hbm,
    cot,
    mesh_out,
    grid_grad,
    dst_out,
    dst_in,
    msg_out,
    msg_in,
    part_out,
    part_in,
    halo_out,
    halo_in,
    back_out,
    back_in,
    gath_out,
    gath_in,
    slot_out,
    slot_in,
    pick,
    scat,
    edge_pick,
    halo_pick,
    act_slope,
    joined,
    far_part,
    feat,
    enc_w,
    mesh_w,
    proc_w,
    load_sem,
    far_grad,
    piece,
    last_part,
    send_sem,
    recv_sem,
):
    sect = lax.axis_index("sect")
    node = lax.axis_index("node")
    world = sects * nodes
    zero = lax.div(sect, sects)
    line = sect * nodes + node
    fanout, grid_rows = length.shape
    degree, block = sources.shape
    width = feat.shape[1]
    whole = block * sects
    cap = msg_out.shape[2]
    slots = nodes * cap
    chunks = msg_out.shape[0]
    part = width // chunks
    layers = proc_w.shape[0]
    fan = halo_out.shape[2]
    halo = world * fan
    span = nodes * fan

    loads = [
        pltpu.make_async_copy(feat_hbm, feat, load_sem.at[0]),
        pltpu.make_async_copy(enc_hbm, enc_w, load_sem.at[1]),
        pltpu.make_async_copy(mesh_hbm, mesh_w, load_sem.at[2]),
        pltpu.make_async_copy(proc_hbm, proc_w, load_sem.at[3]),
    ]
    for load in loads:
        load.start()

    barrier = pltpu.get_barrier_semaphore()

    def greet_node(step, carry):
        peer = lax.rem(node + step, nodes)
        pl.semaphore_signal(barrier, inc=1, device_id=(sect, peer), device_id_type=MESH)
        return carry

    def greet_sect(step, carry):
        peer = lax.rem(sect + step, sects)
        pl.semaphore_signal(barrier, inc=1, device_id=(peer, node), device_id_type=MESH)
        return carry

    lax.fori_loop(1, nodes, greet_node, 0)
    lax.fori_loop(1, sects, greet_sect, 0)

    def push(src, dst, at, device):
        pltpu.make_async_remote_copy(
            src_ref=src,
            dst_ref=dst,
            send_sem=send_sem.at[at],
            recv_sem=recv_sem.at[at],
            device_id=device,
            device_id_type=MESH,
        ).start()

    def over_nodes(src, dst, at):
        def step(off, carry):
            peer = lax.rem(node + off, nodes)
            push(src.at[peer], dst.at[node], at, (sect, peer))
            return carry

        lax.fori_loop(1, nodes, step, 0, unroll=9)

    def over_sect(src, dst, at, peer_sect, first):
        def step(off, carry):
            peer = lax.rem(node + off, nodes)
            push(src.at[peer_sect * nodes + peer], dst.at[line], at, (peer_sect, peer))
            return carry

        lax.fori_loop(int(first), nodes, step, 0, unroll=9 if first else 8)

    def landed(ref, count, sem):
        some = ref.at[pl.ds(0, count)]
        pltpu.make_async_copy(some, some, sem).wait()

    at_dst = 0
    at_msg = 1
    at_part = at_msg + chunks
    at_halo = at_part + chunks
    at_back = at_halo + layers * sects
    at_gath = at_back + layers
    at_slot = at_gath + chunks

    upper = (iota((grid_rows, grid_rows), 0) < iota((grid_rows, grid_rows), 1)).astype(BF16)
    used = jnp.zeros((nodes, 1), F32)
    hots, ranks, columns = [], [], []
    for k in range(fanout):
        own_row = owner[k : k + 1, :]
        hot = (iota((nodes, grid_rows), 0) == own_row).astype(F32)
        before = dot(hot.astype(BF16), upper) + used
        rank = jnp.sum(hot * before, axis=0, keepdims=True).astype(jnp.int32)
        used = used + jnp.sum(hot, axis=1, keepdims=True)
        place = own_row * cap + rank
        pick[:, k * grid_rows : (k + 1) * grid_rows] = (
            iota((slots, grid_rows), 0) == place
        ).astype(BF16)
        hots.append(hot)
        ranks.append(rank)
        columns.append(jnp.broadcast_to(length[k : k + 1, :], (8, grid_rows)).T[:, 0:1])

    for load in loads[:2]:
        load.wait()
    for c in range(chunks):
        cols = slice(c * part, (c + 1) * part)
        pre = dot(feat[...], enc_w[:, cols])
        message = []
        for k in range(fanout):
            act = pre + columns[k] * vec[:, cols]
            sig = jax.nn.sigmoid(act)
            message.append((act * sig).astype(BF16))
            act_slope[k, :, cols] = slope_of(act, sig)
        message = jnp.concatenate(message, axis=0)
        msg_out[c] = dot(pick[...], message).astype(BF16).reshape(nodes, cap, part)
        if c == 0:
            pl.semaphore_wait(barrier, nodes + sects - 2)
        over_nodes(msg_out.at[c], msg_in.at[c], at_msg + c)
        msg_in[c, node] = msg_out[c, node]
        if c == 0:
            table = jnp.zeros((nodes, LANES), F32)
            for k in range(fanout):
                dst_row = dest[k : k + 1, :]
                level = (iota((LANES, grid_rows), 0) == ranks[k]).astype(BF16)
                high = (hots[k] * (dst_row >> 4).astype(F32)).astype(BF16)
                low = (hots[k] * ((dst_row & 15) + 1).astype(F32)).astype(BF16)
                table = table + 16.0 * dot(high, level, NT) + dot(low, level, NT)
            dst_out[...] = table.reshape(nodes, 1, LANES)
            over_nodes(dst_out, dst_in, at_dst)
            dst_in[node] = dst_out[node]

    for k in range(degree):
        edge_pick[:, k * block : (k + 1) * block] = (
            iota((block + halo, block), 0) == sources[k : k + 1, :]
        ).astype(BF16)
    order = iota((nodes, halo), 1)
    spread = (lax.rem(lax.div(order, fan), nodes) == iota((nodes, halo), 0)).astype(BF16)
    order = iota((sects * fan, halo), 1)
    mine = lax.div(order, fan * nodes) * fan + lax.rem(order, fan) == iota(order.shape, 0)
    wide = dot(sends[...].astype(F32).astype(BF16), spread)
    sent = jnp.sum(jnp.where(mine, wide, 0.0), axis=0, keepdims=True).astype(jnp.int32)
    halo_pick[...] = (iota((block, halo), 0) == sent).astype(BF16)

    landed(dst_in, nodes - 1, recv_sem.at[at_dst])
    got = dst_in[...].reshape(nodes, LANES)
    got_high = jnp.floor(got * (1.0 / 16.0))
    got_low = got - 16.0 * got_high
    spread = (lax.rem(iota((LANES, slots), 1), cap) == iota((LANES, slots), 0)).astype(BF16)
    mine = (lax.div(iota((nodes, slots), 1), cap) == iota((nodes, slots), 0)).astype(F32)
    wide = 16.0 * dot(got_high.astype(BF16), spread) + dot(got_low.astype(BF16), spread)
    got_row = jnp.sum(wide * mine, axis=0, keepdims=True).astype(jnp.int32) - 1
    scat[...] = (iota((whole, slots), 0) == got_row).astype(BF16)

    mesh_pre = jnp.zeros((block, width), F32)
    for load in loads[2:]:
        load.wait()
    for c in range(chunks):
        landed(msg_in.at[c], nodes - 1, recv_sem.at[at_msg + c])
        agg = dot(scat[...], msg_in[c].reshape(slots, part))
        part_out[c] = agg.astype(BF16).reshape(sects, block, part)
        for off in range(1, sects):
            peer = lax.rem(sect + off, sects)
            push(part_out.at[c, peer], part_in.at[c, sect], at_part + c, (peer, node))
        part_in[c, sect] = part_out[c, sect]
    for c in range(chunks):
        landed(part_in.at[c], sects - 1, recv_sem.at[at_part + c])
        total = jnp.sum(part_in[c].astype(F32), axis=0)
        last_part[c, :block, :] = dot(total.astype(BF16), mesh_w[c * part : (c + 1) * part, :])
    for c in range(chunks):
        mesh_pre = mesh_pre + last_part[zero + c, :block, :]
    mesh_sig = jax.nn.sigmoid(mesh_pre)
    state = (init[...].astype(F32) + mesh_pre * mesh_sig).astype(BF16)

    saved = []
    for layer in range(layers):
        for off in range(sects):
            peer = lax.rem(sect + off, sects)
            cols = pl.ds(pl.multiple_of(peer * span, span), span)
            out = dot(halo_pick[:, cols], state, TN).astype(BF16)
            halo_out[layer, pl.ds(peer * nodes, nodes)] = out.reshape(nodes, fan, width)
            over_sect(halo_out.at[layer], halo_in.at[layer], at_halo + layer * sects + off, peer, off == 0)
        halo_in[layer, line] = halo_out[layer, line]
        near = dot(edge_pick[:block, :], state, TN).astype(BF16)
        piece[2] = dot(state, proc_w[layer, 1])
        joined[layer] = dot(near, proc_w[layer, 0])
        piece[1] = dot(state, proc_w[layer, 2])
        if layer > 0:
            prev = joined[layer - 1]
            joined[layer - 1] = slope_of(prev, jax.nn.sigmoid(prev))
        every = pl.ds(pl.multiple_of(zero * block, block), degree * block)
        for off in range(sects):
            peer = lax.rem(sect + sects - off, sects)
            landed(
                halo_in.at[layer, pl.ds(peer * nodes, nodes)],
                nodes - int(off == 0),
                recv_sem.at[at_halo + layer * sects + off],
            )
            rows = pl.ds(pl.multiple_of(block + peer * span, span), span)
            incoming = halo_in[layer, pl.ds(peer * nodes, nodes)].reshape(span, width)
            found = dot(edge_pick[rows, :], incoming, TN)
            far_part[...] = found if off == 0 else far_part[every, :] + found
        far_rows = far_part[every, :].astype(BF16)
        agg = jnp.zeros((block, width), F32)
        to_dst = piece[zero + 2]
        for k in range(degree):
            if k % (degree // 2) == 0:
                some = slice(k * block, (k + degree // 2) * block)
                far_part[some, :] = dot(far_rows[some, :], proc_w[layer, 0])
            rows = slice(k * block, (k + 1) * block)
            full = joined[zero + layer, rows, :] + far_part[rows, :] + to_dst
            gate = jax.nn.sigmoid(full)
            joined[layer, rows, :] = full if layer < layers - 1 else slope_of(full, gate)
            agg = agg + full * gate
        agg = agg.astype(BF16)
        piece[0] = dot(agg, proc_w[layer, 3])
        mixed = piece[zero + 1] + piece[zero]
        centred = mixed - jnp.mean(mixed, axis=1, keepdims=True)
        scale = lax.rsqrt(jnp.mean(centred * centred, axis=1, keepdims=True) + 1e-05)
        normed = centred * scale
        sig = jax.nn.sigmoid(normed)
        saved.append((normed, scale, slope_of(normed, sig)))
        state = (state.astype(F32) + normed * sig).astype(BF16)
    mesh_out[...] = state

    grad = cot[...].astype(F32)
    for layer in reversed(range(layers)):
        normed, scale, slope = saved[layer]
        grad_normed = grad * slope
        grad_mixed = scale * (
            grad_normed
            - jnp.mean(grad_normed, axis=1, keepdims=True)
            - normed * jnp.mean(grad_normed * normed, axis=1, keepdims=True)
        )
        grad_mixed = grad_mixed.astype(BF16)
        grad_agg = dot(grad_mixed, proc_w[layer, 3], NT)
        grad_dst = jnp.zeros((block, width), F32)
        for k in range(degree):
            rows = slice(k * block, (k + 1) * block)
            grad_joined = joined[layer, rows, :] * grad_agg
            grad_dst = grad_dst + grad_joined
            far_grad[rows, :] = grad_joined.astype(BF16)
        grad_dst = grad_dst.astype(BF16)
        for off in range(sects):
            peer = lax.rem(sect + off, sects)
            rows = pl.ds(pl.multiple_of(block + peer * span, span), span)
            out = dot(edge_pick[rows, :], far_grad[...]).astype(BF16)
            back_out[layer, pl.ds(peer * nodes, nodes)] = out.reshape(nodes, fan, width)
            over_sect(back_out.at[layer], back_in.at[layer], at_back + layer, peer, off == 0)
        back_in[layer, line] = back_out[layer, line]
        piece[0] = dot(grad_mixed, proc_w[layer, 2], NT)
        piece[1] = dot(grad_dst, proc_w[layer, 1], NT)
        piece[2] = dot(edge_pick[:block, :], far_grad[...])
        landed(back_in.at[layer], world - 1, recv_sem.at[at_back + layer])
        piece[3] = dot(halo_pick[...], back_in[layer].reshape(halo, width))
        grad_src = (piece[zero + 2] + piece[zero + 3]).astype(BF16)
        piece[4] = dot(grad_src, proc_w[layer, 0], NT)
        grad = grad + piece[zero] + piece[zero + 1] + piece[zero + 4]

    grad_pre = (grad * slope_of(mesh_pre, mesh_sig)).astype(BF16)
    for c in range(chunks):
        cols = slice(c * part, (c + 1) * part)
        gath_out[c] = dot(grad_pre, mesh_w[cols, :], NT).astype(BF16)
        for off in range(1, sects):
            peer = lax.rem(sect + off, sects)
            push(gath_out.at[c], gath_in.at[c, sect], at_gath + c, (peer, node))
        gath_in[c, sect] = gath_out[c]
    for c in range(chunks):
        landed(gath_in.at[c], sects - 1, recv_sem.at[at_gath + c])
        rows = dot(scat[...], gath_in[c].reshape(whole, part), TN).astype(BF16)
        slot_out[c] = rows.reshape(nodes, cap, part)
        over_nodes(slot_out.at[c], slot_in.at[c], at_slot + c)
        slot_in[c, node] = slot_out[c, node]
    for c in range(chunks):
        cols = slice(c * part, (c + 1) * part)
        landed(slot_in.at[c], nodes - 1, recv_sem.at[at_slot + c])
        back = dot(pick[...], slot_in[c].reshape(slots, part), TN)
        grad_act = jnp.zeros((grid_rows, part), F32)
        for k in range(fanout):
            grad_act = grad_act + (
                back[k * grid_rows : (k + 1) * grid_rows] * act_slope[k, :, cols]
            )
        last_part[c] = dot(grad_act.astype(BF16), enc_w[:, cols], NT)
    total = last_part[zero]
    for c in range(1, chunks):
        total = total + last_part[zero + c]
    grid_grad[...] = total.astype(BF16)

    landed(dst_out, nodes - 1, send_sem.at[at_dst])
    for c in range(chunks):
        landed(msg_out.at[c], nodes - 1, send_sem.at[at_msg + c])
        landed(part_out.at[c], sects - 1, send_sem.at[at_part + c])
        landed(gath_in.at[c], sects - 1, send_sem.at[at_gath + c])
        landed(slot_out.at[c], nodes - 1, send_sem.at[at_slot + c])
    for layer in range(layers):
        for off in range(sects):
            peer = lax.rem(sect + off, sects)
            landed(
                halo_out.at[layer, pl.ds(peer * nodes, nodes)],
                nodes - int(off == 0),
                send_sem.at[at_halo + layer * sects + off],
            )
        landed(back_out.at[layer], world - 1, send_sem.at[at_back + layer])


def finish(state, grad, mesh_out, grid_grad):
    mesh_out[...] = state[...]
    grid_grad[...] = grad[...]


def body(
    grid_feat,
    edge_len,
    g2m_owner,
    g2m_dst,
    enc_weight,
    enc_vec,
    mesh_init,
    mesh_weight,
    halo_send,
    mesh_src,
    proc_weight,
    cot,
):
    nodes = lax.axis_size("node")
    sects = lax.axis_size("sect")
    world = nodes * sects
    grid_rows, width = grid_feat.shape
    fanout = edge_len.shape[1]
    cap = max(2, 2 * grid_rows * fanout // nodes)
    block = mesh_init.shape[1]
    fan = halo_send.shape[4]
    layers = proc_weight.shape[0]
    degree = mesh_src.shape[2]
    slots = nodes * cap
    chunks = CHUNKS
    part = width // chunks
    whole = block * sects
    count = 1 + 4 * chunks + (1 + sects) * layers
    vmem = pl.BlockSpec(memory_space=pltpu.VMEM)
    hbm = pl.BlockSpec(memory_space=pl.ANY)
    out_shape = (
        jax.ShapeDtypeStruct((block, width), BF16),
        jax.ShapeDtypeStruct((grid_rows, width), BF16),
    )
    out = pl.pallas_call(
        functools.partial(fused, sects, nodes),
        out_shape=out_shape,
        in_specs=[hbm, vmem, vmem, vmem, hbm, vmem, vmem, hbm, vmem, vmem, hbm, vmem],
        out_specs=(vmem, vmem),
        scratch_shapes=[
            pltpu.VMEM((nodes, 1, LANES), F32),
            pltpu.VMEM((nodes, 1, LANES), F32),
            pltpu.VMEM((chunks, nodes, cap, part), BF16),
            pltpu.VMEM((chunks, nodes, cap, part), BF16),
            pltpu.VMEM((chunks, sects, block, part), BF16),
            pltpu.VMEM((chunks, sects, block, part), BF16),
            pltpu.VMEM((layers, world, fan, width), BF16),
            pltpu.VMEM((layers, world, fan, width), BF16),
            pltpu.VMEM((layers, world, fan, width), BF16),
            pltpu.VMEM((layers, world, fan, width), BF16),
            pltpu.VMEM((chunks, block, part), BF16),
            pltpu.VMEM((chunks, sects, block, part), BF16),
            pltpu.VMEM((chunks, nodes, cap, part), BF16),
            pltpu.VMEM((chunks, nodes, cap, part), BF16),
            pltpu.VMEM((slots, fanout * grid_rows), BF16),
            pltpu.VMEM((whole, slots), BF16),
            pltpu.VMEM((block + world * fan, degree * block), BF16),
            pltpu.VMEM((block, world * fan), BF16),
            pltpu.VMEM((fanout, grid_rows, width), F32),
            pltpu.VMEM((layers, degree * block, width), F32),
            pltpu.VMEM((degree * block, width), F32),
            pltpu.VMEM(grid_feat.shape, BF16),
            pltpu.VMEM(enc_weight.shape, BF16),
            pltpu.VMEM(mesh_weight.shape, BF16),
            pltpu.VMEM(proc_weight.shape, BF16),
            pltpu.SemaphoreType.DMA((4,)),
            pltpu.VMEM((degree * block, width), BF16),
            pltpu.VMEM((5, block, width), F32),
            pltpu.VMEM((chunks, grid_rows, width), F32),
            pltpu.SemaphoreType.DMA((count,)),
            pltpu.SemaphoreType.DMA((count,)),
        ],
        compiler_params=pltpu.CompilerParams(
            collective_id=0, has_side_effects=True, vmem_limit_bytes=60 * 2**20
        ),
        name="grid_mesh",
    )(
        grid_feat,
        edge_len.T,
        g2m_owner.T,
        g2m_dst.T,
        enc_weight,
        enc_vec.reshape(1, width),
        mesh_init[0],
        mesh_weight,
        halo_send[0, 0].transpose(0, 2, 1).reshape(sects * fan, nodes),
        mesh_src[0].T,
        proc_weight,
        cot[0],
    )
    out = pl.pallas_call(
        finish,
        out_shape=out_shape,
        in_specs=[vmem] * 2,
        out_specs=(vmem, vmem),
        name="finish",
    )(*out)
    return (out[0][None], out[1])


def solution(mesh):
    return jax.shard_map(
        body,
        mesh=mesh,
        in_specs=(
            P(("sect", "node"), None),
            P(("sect", "node"), None),
            P(("sect", "node"), None),
            P(("sect", "node"), None),
            P(),
            P(),
            P("node", "sect", None),
            P(),
            P("sect", "node", None, None, None),
            P("node", "sect", None),
            P(),
            P("node", "sect", None),
        ),
        out_specs=(P("node", "sect", None), P(("sect", "node"), None)),
        check_vma=False,
    )
```
